128 devices in a mesh: section: 8 (over z, core), dp: 16 (over y, x).
Axes of the slice: x: 4, y: 4, z: 4, core: 2. Of those that a mesh axis runs over, the one named last changes fastest.
Arguments:
- step_rows: bfloat16 [3, 16, 16, 8192], P(None, None, 'dp'), may hold values from -6 to 6
- cache: bfloat16 [8, 16, 16, 32, 2048], P('section', None, 'dp'), may hold values from -400 to 400
- new_kv: bfloat16 [8, 3, 16, 16, 2048], P('section', None, None, 'dp'), may hold values from -6 to 6
- gains: bfloat16 [8, 8192], P('section'), may hold values from 0.25 to 1.75
- parents: int32 [3, 16, 16, 1], replicated, may hold values from 0 to 15; in each aligned block of 8 rows (0 to 7, 8 to 15, ..., all dimensions but the last counted through in order) no two rows name the same one
Outputs:
- layer_rows: bfloat16 [8, 3, 16, 16, 8192], P('section', None, None, 'dp')
- cache_out: bfloat16 [8, 16, 16, 32, 2048], P('section', None, 'dp')
The draws below stay inside these ranges and needn't reach their ends.
Inputs may be any that keep to these rules, and one draw needn't show every extreme that they name: Within each aligned block of 8 requests, the parents of one beam at one step are distinct beams.
All inputs are finite; a program needn't handle non-finite values.
Results may differ from the reference program's by a relative error of at most 0.02.
Values may be sent and summed in bfloat16 or wider, within the bound.
No kernel may reach another device: no remote copies, remote signals or barrier semaphores. Data moves between devices by JAX's collectives and lax.ppermute only.
A program may use at most 64 MiB of HBM per device.

```python
import math
import jax
import jax.numpy as jnp
import numpy as np
from jax import lax

D = 8192
HEADS = 64
KVH = 8
HD = 128
STEPS = 3
REQS = 16
LEN = 32
BEAMS = 16
LAYERS = 8
KV2 = 2048


def draw_cache(key, part):
    key = jax.random.fold_in(key, 5)
    shape = (LAYERS, REQS, BEAMS, LEN, 2 * KVH * HD)
    base = jnp.clip(jax.random.normal(key, shape, jnp.float32), -5.0, 5.0)
    return base.astype(jnp.bfloat16)


def steps_of(key, shape, pieces, smallest, high):
    factor_of, own = 1.0, jax.random.fold_in(key, 6)
    for axis_at, parts in pieces:
        steps = jnp.exp(jax.random.uniform(jax.random.fold_in(own, axis_at), (parts,), jnp.float32, smallest / len(pieces), high / len(pieces)))
        factor_of = factor_of * jnp.repeat(steps, shape[axis_at] // parts).reshape([-1 if axis == axis_at else 1 for axis in range(len(shape))])
    return factor_of


def deal_out(own_key, own, number, rows, amount, top, bound, skew):
    ranking = jax.random.permutation(own_key, amount)
    crowded, common = portions_of(amount, rows * top, bound, skew, True), portions_of(amount, rows * top, bound, skew, False)
    places = jnp.arange(amount)

    def named(lengths, offset_by):
        used = int((lengths > 0).sum())
        fixed = max(1, used // 4)
        shifted = fixed + (places - fixed + offset_by * (used - fixed)) % max(1, amount - fixed)
        return jnp.zeros((amount,), jnp.int32).at[ranking[jnp.where(places < fixed, places, shifted)]].set(jnp.asarray(lengths, jnp.int32))

    lengths = jnp.where(number % 4 == 0, named(crowded, number // 4), named(common, number - number // 4 - 1))
    mixed = jax.random.permutation(jax.random.fold_in(own, 3), amount)
    source_of, sink = mixed[0:amount // 2 * 2:2], mixed[1:amount // 2 * 2:2]
    margin = jnp.minimum(lengths[source_of] - 1, bound - lengths[sink]) // 2
    margin = jnp.where((source_of == ranking[0]) | (sink == ranking[0]) | (lengths[sink] == 0), 0, jnp.maximum(margin, 0))
    shifted = jax.random.randint(jax.random.fold_in(own, 4), (amount // 2,), 0, 1 << 20) % (margin + 1)
    lengths = lengths.at[source_of].add(-shifted).at[sink].add(shifted)
    items = jnp.searchsorted(jnp.cumsum(lengths), jnp.arange(rows * top), side="right").astype(jnp.int32)
    grid = items.reshape(top, rows).T
    grid = grid[jax.random.permutation(jax.random.fold_in(own, 1), rows)]
    offset_by = jax.random.randint(jax.random.fold_in(own, 2), (rows, 1), 0, top)
    return jnp.take_along_axis(grid, (jnp.arange(top)[None, :] + offset_by) % top, axis=1)


def portions_of(number_of, total, reach, slope, full):
    loads = [(1 << 20) // math.isqrt(grade ** slope) + 1 for grade in range(1, number_of + 1)]
    largest = reach if full else min(reach, max(-(-total // number_of), total * loads[0] // sum(loads)))
    least = 1 if total - largest >= number_of - 1 else 0
    given, rest = [largest] + [least] * (number_of - 1), total - largest - least * (number_of - 1)
    while rest > 0:
        free = [i for i in range(1, number_of) if given[i] < largest] or [i for i in range(1, number_of) if given[i] < reach]
        whole, remaining = sum([loads[i] for i in free]), rest
        for i in free:
            addition = min(reach - given[i], max(1, remaining * loads[i] // whole), rest)
            given[i] = given[i] + addition
            rest = rest - addition
    return np.array(given)


def scatter_about(stream_key, shape, deviation, bound, cuts=(), dtype=jnp.bfloat16):
    level = steps_of(stream_key, shape, cuts, -0.22, 0.18) if cuts else 1.0
    array = jax.random.normal(stream_key, shape, jnp.float32) * deviation * level
    return jnp.minimum(jnp.maximum(array, -bound), bound).astype(dtype)


def setup_inputs(seed: int = 0) -> dict:
    arg_keys = jax.random.split(jax.random.key(seed), 6)
    step_rows = scatter_about(arg_keys[0], (STEPS, REQS, BEAMS, D), 1.0, 6.0, ((2, 16),))
    cache = draw_cache(jax.random.fold_in(arg_keys[5], 71), 0)
    new_kv = scatter_about(arg_keys[2], (LAYERS, STEPS, REQS, BEAMS, KV2), 1.0, 6.0, ((0, 8), (3, 16)))
    gains = jnp.clip(1.0 + 0.15 * jax.random.normal(arg_keys[3], (LAYERS, D), jnp.float32), 0.25, 1.75).astype(jnp.bfloat16)
    parents_keys = jax.random.split(jax.random.fold_in(arg_keys[4], 1), STEPS * BEAMS * REQS // 8)
    parents_turns = jax.random.permutation(jax.random.fold_in(arg_keys[4], 3), STEPS * BEAMS * REQS // 8)
    parents = jax.vmap(lambda own, number: deal_out(jax.random.fold_in(arg_keys[4], 2), own, number, 8, BEAMS, 1, 1, 2))(parents_keys, parents_turns).reshape((STEPS, BEAMS, REQS, 1))
    return {"step_rows": step_rows, "cache": cache, "new_kv": new_kv, "gains": gains, "parents": parents}


def layer(rows, slots, gain, pos):
    x = rows.astype(jnp.float32)
    scale = jax.lax.rsqrt(lax.optimization_barrier(jnp.mean(x * x, axis=-1, keepdims=True)) + 1e-05)
    query = (x * scale * gain.astype(jnp.float32)).astype(jnp.bfloat16).astype(jnp.float32)
    lead = rows.shape[:-1]
    query = query.reshape(lead + (KVH, HEADS // KVH, HD))
    keys = slots[..., :KVH * HD].astype(jnp.float32).reshape(lead + (LEN, KVH, HD))
    values = slots[..., KVH * HD:].astype(jnp.float32).reshape(lead + (LEN, KVH, HD))
    scores = jnp.einsum('rbkgd,rblkd->rbkgl', query, keys) * HD ** (-0.5)
    live = jnp.arange(LEN) <= pos
    scores = jnp.where(live, scores, -1e+30)
    top = lax.optimization_barrier(jnp.max(scores, axis=-1, keepdims=True))
    expo = jnp.exp(scores - top)
    weights = (expo / lax.optimization_barrier(jnp.sum(expo, axis=-1, keepdims=True))).astype(jnp.bfloat16).astype(jnp.float32)
    attended = jnp.einsum('rbkgl,rblkd->rbkgd', weights, values).reshape(lead + (D,))
    return (x + attended).astype(jnp.bfloat16)

def reference(step_rows, cache, new_kv, gains, parents):
    start = LEN - STEPS
    requests = jnp.arange(REQS)[:, None]
    per_step = []
    for step in range(STEPS):
        chosen = parents[step, :, :, 0].T
        cache = cache[:, requests, chosen]
        cache = cache.at[:, :, :, start + step].set(new_kv[:, step])
        rows = step_rows[step]
        outputs = []
        for level in range(LAYERS):
            rows = layer(rows, cache[level], gains[level], start + step)
            outputs.append(rows)
        per_step.append(jnp.stack(outputs))
    return (jnp.stack(per_step, axis=1), cache)
```

```python
import functools

import jax
import jax.numpy as jnp
from jax import lax
from jax.experimental import pallas as pl
from jax.experimental.pallas import tpu as pltpu
from jax.sharding import PartitionSpec as P

HEADS = 64
KVH = 8
HD = 128
STEPS = 3
REQS = 16
BEAMS = 16
LEN = 32
PAST = LEN - STEPS
D = HEADS * HD
KV2 = 2 * KVH * HD
HALF = BEAMS // 2
EXTRA = 8
BF = jnp.bfloat16
F32 = jnp.float32
VMEM = pltpu.VMEM
SMEM = pltpu.SMEM


def spec(space):
    return pl.BlockSpec(memory_space=space)


def pack_kernel(which_ref, cache_ref, fresh_ref, rows_ref, out_ref, fresh, flat):
    del which_ref
    for u in range(STEPS):
        fresh[u * REQS : (u + 1) * REQS, :] = fresh_ref[u].astype(F32)
    for a in range(HEADS):
        tile = rows_ref[0, :, a * HD : (a + 1) * HD].astype(F32)
        flat[pl.ds(a, 8, stride=HEADS), :] = tile[:8]
        flat[pl.ds(8 * HEADS + a, 8, stride=HEADS), :] = tile[8:]
    place = lax.broadcasted_iota(jnp.int32, (16, KV2), 0)

    def one(r, _):
        out_ref[r, 0:16, :] = cache_ref[r, 0:16, :]
        late = cache_ref[r, 16:32, :].astype(F32)
        for u in range(STEPS):
            new = fresh[pl.ds(u * REQS + r, 1), :]
            late = jnp.where(place == PAST - 16 + u, new, late)
        out_ref[r, 16:32, :] = late.astype(BF)
        for k in range(8):
            part = flat[pl.ds(pl.multiple_of(r * HEADS + 8 * k, 8), 8), :]
            out_ref[r, LEN : LEN + EXTRA, k * HD : (k + 1) * HD] = part.astype(BF)
        return 0

    lax.fori_loop(0, REQS, one, 0)


def pack(which, slots, fresh, rows):
    return pl.pallas_call(
        pack_kernel,
        out_shape=jax.ShapeDtypeStruct((REQS, LEN + EXTRA, KV2), BF),
        grid_spec=pltpu.PrefetchScalarGridSpec(
            num_scalar_prefetch=1,
            grid=(1,),
            in_specs=[
                pl.BlockSpec((REQS, LEN, KV2), lambda i, w: (0, 0, 0)),
                pl.BlockSpec((STEPS, REQS, KV2), lambda i, w: (0, 0, 0)),
                pl.BlockSpec((1, REQS, D), lambda i, w: (w[0], 0, 0)),
            ],
            out_specs=pl.BlockSpec((REQS, LEN + EXTRA, KV2), lambda i, w: (0, 0, 0)),
            scratch_shapes=[VMEM((STEPS * REQS, KV2), F32), VMEM((REQS * HEADS, HD), F32)],
        ),
        compiler_params=pltpu.CompilerParams(vmem_limit_bytes=24 * 2**20),
        name="pack",
    )(which, slots, fresh, rows)


def first_kernel(idx_ref, extra_ref, out_ref, flat):
    core = idx_ref[1]
    for j in range(HALF):
        for k in range(8):
            part = extra_ref[HALF * core + j, :, k * HD : (k + 1) * HD].astype(F32)
            flat[j * HEADS + 8 * k : j * HEADS + 8 * k + 8, :] = part
    for a in range(HEADS):
        out_ref[:, a * HD : (a + 1) * HD] = flat[pl.ds(a, HALF, stride=HEADS), :].astype(BF)


def first_rows(idx, arrived):
    return pl.pallas_call(
        first_kernel,
        out_shape=jax.ShapeDtypeStruct((HALF, D), BF),
        grid=(1,),
        in_specs=[
            spec(SMEM),
            pl.BlockSpec((BEAMS, EXTRA, D // 8), lambda i: (0, LEN // EXTRA, 0)),
        ],
        out_specs=pl.BlockSpec((HALF, D), lambda i: (0, 0)),
        scratch_shapes=[VMEM((HALF * HEADS, HD), F32)],
        name="first_rows",
    )(idx, arrived)


def parent(par_ref, step, beam, mine):
    return par_ref[step * BEAMS * REQS + beam * REQS + mine]


def tick_kernel(tick, *refs):
    idx_ref, par_ref, gain_own, gain_oth, carry_ref, y_ref, yo_ref = refs[:7]
    refs = refs[7:] if tick == 0 else refs[9:]
    out_ref, r_own, r_oth, buf, bias, h, flat, sent, sems, osems = refs
    stage, core, mine = idx_ref[0], idx_ref[1], idx_ref[2]
    step = tick - stage
    active = (step >= 0) & (step < STEPS)

    @pl.when(jnp.logical_not(active))
    def _():
        out_ref[...] = carry_ref[...]

    @pl.when(active)
    def _():
        pltpu.make_async_copy(y_ref.at[:, pl.ds(0, LEN), :], buf.at[core], sems.at[core]).start()
        other = 1 - core
        pltpu.make_async_copy(yo_ref.at[:, pl.ds(0, LEN), :], buf.at[other], sems.at[other]).start()
        col = lax.broadcasted_iota(jnp.int32, (1, BEAMS * LEN), 1)
        beam, pos = col >> 5, col & (LEN - 1)
        for j in range(HALF):
            me = HALF * core + j
            c2 = jnp.where(step == 2, parent(par_ref, 2, me, mine), me)
            c1 = jnp.where(step >= 1, parent(par_ref, 1, c2, mine), c2)
            root = parent(par_ref, 0, c1, mine)
            second = jnp.where(step >= 1, c2, -1)
            third = jnp.where(step == 2, me, -1)
            want = jnp.where(
                pos < PAST,
                root,
                jnp.where(pos == PAST, c1, jnp.where(pos == PAST + 1, second, third)),
            )
            bias[j : j + 1, :] = jnp.where(beam == want, 0.0, -1e30)
        h[...] = carry_ref[...].astype(F32)
        for layer in range(2):
            pltpu.make_async_copy(
                y_ref.at[:, pl.ds(0, LEN), :], buf.at[layer], sems.at[layer]
            ).wait()
            x = h[...]
            scale = lax.rsqrt(jnp.sum(x * x, axis=1, keepdims=True) * (1.0 / D) + 1e-05)
            pick = jnp.full((1, HD), core, jnp.int32) == layer
            for g in range(KVH):
                heads = [
                    slice((g * KVH + a) * HD, (g * KVH + a + 1) * HD) for a in range(HEADS // KVH)
                ]
                query = jnp.concatenate(
                    [
                        h[:, s]
                        * scale
                        * jnp.where(pick, gain_own[:, s].astype(F32), gain_oth[:, s].astype(F32))
                        for s in heads
                    ],
                    axis=0,
                ).astype(BF)
                keys = buf[layer, :, :, g * HD : (g + 1) * HD].reshape(BEAMS * LEN, HD)
                values = buf[layer, :, :, (KVH + g) * HD : (KVH + g + 1) * HD].reshape(
                    BEAMS * LEN, HD
                )
                scores = lax.dot_general(
                    query, keys, (((1,), (1,)), ((), ())), preferred_element_type=F32
                )
                scores = scores.reshape(HEADS // KVH, HALF, BEAMS * LEN) * HD ** (-0.5)
                scores = scores + bias[...][None]
                top = jnp.max(scores, axis=-1, keepdims=True)
                expo = jnp.exp(scores - top)
                weights = expo * (1.0 / jnp.sum(expo, axis=-1, keepdims=True))
                weights = weights.reshape(HEADS, BEAMS * LEN).astype(BF)
                attended = jnp.dot(weights, values, preferred_element_type=F32)
                for a, s in enumerate(heads):
                    total = (h[:, s] + attended[a * HALF : (a + 1) * HALF]).astype(BF)
                    h[:, s] = total.astype(F32)
                    flat[pl.ds(g * KVH + a, HALF, stride=HEADS), :] = total.astype(F32)
            sent[layer] = flat[...].astype(BF).reshape(HALF, HEADS, HD)

            @pl.when(core == layer)
            def _():
                pltpu.make_async_copy(sent.at[layer], r_own.at[:, step], osems.at[layer]).start()

            @pl.when(core != layer)
            def _():
                pltpu.make_async_copy(sent.at[layer], r_oth.at[:, step], osems.at[layer]).start()

        out_ref[...] = h[...].astype(BF)
        for layer in range(2):
            pltpu.make_async_copy(sent.at[layer], r_own.at[:, step], osems.at[layer]).wait()


def run_tick(tick, idx, par, gain_own, gain_oth, carry, y, yo, records):
    record = jax.ShapeDtypeStruct((HALF, STEPS, HEADS, HD), BF)
    return pl.pallas_call(
        functools.partial(tick_kernel, tick),
        out_shape=(jax.ShapeDtypeStruct((HALF, D), BF), record, record),
        in_specs=[spec(SMEM), spec(SMEM), spec(VMEM), spec(VMEM), spec(VMEM)]
        + [spec(pl.ANY)] * (2 + len(records)),
        out_specs=(spec(VMEM), spec(pl.ANY), spec(pl.ANY)),
        scratch_shapes=[
            VMEM((2, BEAMS, LEN, KV2), BF),
            VMEM((HALF, BEAMS * LEN), F32),
            VMEM((HALF, D), F32),
            VMEM((HALF * HEADS, HD), F32),
            VMEM((2, HALF, HEADS, HD), BF),
            pltpu.SemaphoreType.DMA((2,)),
            pltpu.SemaphoreType.DMA((2,)),
        ],
        input_output_aliases={7: 1, 8: 2} if records else {},
        compiler_params=pltpu.CompilerParams(vmem_limit_bytes=24 * 2**20),
        cost_estimate=pl.CostEstimate(flops=10**8, bytes_accessed=5 * 2**20, transcendentals=0),
        name="tick",
    )(idx, par, gain_own, gain_oth, carry, y, yo, *records)


GROUP = 4


def reorder_kernel(idx_ref, par_ref, y_ref, out_ref):
    mine = idx_ref[2]
    place = lax.broadcasted_iota(jnp.int32, (16, KV2), 0)

    def one(i, _):
        j = pl.program_id(0) * GROUP + i
        c2 = parent(par_ref, 2, j, mine)
        c1 = parent(par_ref, 1, c2, mine)
        root = parent(par_ref, 0, c1, mine)
        out_ref[i, 0:16, :] = y_ref[root, 0:16, :]
        late = y_ref[root, 16:32, :].astype(F32)
        for u, source in enumerate((c1, c2, j)):
            late = jnp.where(place == PAST - 16 + u, y_ref[source, 16:32, :].astype(F32), late)
        out_ref[i, 16:32, :] = late.astype(BF)
        return 0

    lax.fori_loop(0, GROUP, one, 0)


def reorder(idx, par, y):
    return pl.pallas_call(
        reorder_kernel,
        out_shape=jax.ShapeDtypeStruct((BEAMS, LEN, KV2), BF),
        grid=(BEAMS // GROUP,),
        in_specs=[
            spec(SMEM),
            spec(SMEM),
            pl.BlockSpec((BEAMS, LEN + EXTRA, KV2), lambda i: (0, 0, 0)),
        ],
        out_specs=pl.BlockSpec((GROUP, LEN, KV2), lambda i: (i, 0, 0)),
        compiler_params=pltpu.CompilerParams(vmem_limit_bytes=24 * 2**20),
        cost_estimate=pl.CostEstimate(flops=10**6, bytes_accessed=5 * 2**20, transcendentals=0),
        name="reorder",
    )(idx, par, y)


def spread_kernel(in_ref, out_ref, flat):
    for r in range(REQS):
        flat[r * HEADS : (r + 1) * HEADS, :] = in_ref[r, 0].astype(F32)
    for a in range(HEADS):
        low = flat[pl.ds(a, 8, stride=HEADS), :]
        high = flat[pl.ds(8 * HEADS + a, 8, stride=HEADS), :]
        out_ref[0, :, a * HD : (a + 1) * HD] = jnp.concatenate([low, high], axis=0).astype(BF)


def spread(arrived):
    return pl.pallas_call(
        spread_kernel,
        out_shape=jax.ShapeDtypeStruct((STEPS, REQS, D), BF),
        grid=(STEPS,),
        in_specs=[pl.BlockSpec((REQS, 1, HEADS, HD), lambda t: (0, t, 0, 0))],
        out_specs=pl.BlockSpec((1, REQS, D), lambda t: (t, 0, 0)),
        scratch_shapes=[VMEM((REQS * HEADS, HD), F32)],
        name="spread",
    )(arrived)


def on_device(step_rows, cache, new_kv, gains, parents):
    sections = lax.axis_size("section")
    section = lax.axis_index("section")
    stage, core = section // 2, section % 2
    swap = [(i, i ^ 1) for i in range(sections)]
    ahead = [(i, (i + 2) % sections) for i in range(sections)]
    idx = jnp.stack([stage, core, lax.axis_index("dp")]).astype(jnp.int32)
    par = parents.reshape(-1)
    which = jnp.minimum((sections // 2 - stage) % (sections // 2), STEPS - 1)
    which = which.astype(jnp.int32).reshape(1)
    gain_own = gains
    gain_oth = lax.ppermute(gains, "section", swap)

    packed = pack(which, cache[0, :, 0], new_kv[0, :, :, 0], step_rows[:, :, 0])
    y = lax.all_to_all(packed, "dp", split_axis=0, concat_axis=0, tiled=True)
    yo = lax.ppermute(y, "section", swap)
    carry = first_rows(idx, y)
    back = reorder(idx, par, y)
    cache_out = lax.all_to_all(back, "dp", split_axis=0, concat_axis=0, tiled=True)

    records = ()
    ticks = STEPS + sections // 2 - 1
    for tick in range(ticks):
        carry, *records = run_tick(tick, idx, par, gain_own, gain_oth, carry, y, yo, records)
        if tick < ticks - 1:
            carry = lax.ppermute(carry, "section", ahead)
    own, oth = records
    oth = lax.ppermute(oth, "section", swap)
    rows = jnp.where(
        core == 0, jnp.concatenate([own, oth], axis=0), jnp.concatenate([oth, own], axis=0)
    )
    rows = lax.all_to_all(rows, "dp", split_axis=0, concat_axis=0, tiled=True)
    rows = spread(rows)
    return (rows[None, :, :, None], cache_out[None, :, None])


def solution(mesh):
    return jax.shard_map(
        on_device,
        mesh=mesh,
        in_specs=(
            P(None, None, "dp", None),
            P("section", None, "dp", None, None),
            P("section", None, None, "dp", None),
            P("section", None),
            P(),
        ),
        out_specs=(P("section", None, None, "dp", None), P("section", None, "dp", None, None)),
        check_vma=False,
    )
```
